32 devices in a mesh: ep: 16 (over z, y, core), dp: 2 (over x).
Axes of the slice: x: 2, y: 2, z: 4, core: 2. Of those that a mesh axis runs over, the one named last changes fastest.
Arguments:
- out_grad: bfloat16 [4096, 3584], P(('ep', 'dp')), may hold values from -6 to 6
- expert_ids: int32 [4096, 2], P(('ep', 'dp')), may hold values from 0 to 15, all different within a row; in each aligned block of 128 rows (0 to 127, 128 to 255, ...) at most 24 rows name the same one
- combine: float32 [4096, 2], P(('ep', 'dp')), may hold values from 0.1 to 1
- router_logits: bfloat16 [4096, 384], P(('ep', 'dp')), may hold values from -16 to 250
- saved_hidden: bfloat16 [16, 768, 1024], P('ep', 'dp'), may hold values from -6 to 6
- weight: bfloat16 [16, 1024, 3584], P('ep', 'dp'), may hold values from -0.1875 to 0.1875
- moment_one: bfloat16 [16, 1024, 3584], P('ep', 'dp'), may hold values from -6 to 6
- moment_two: bfloat16 [16, 1024, 3584], P('ep', 'dp'), may hold values from 2 to 40
- next_hidden: bfloat16 [16, 64, 1024], P('ep', 'dp'), may hold values from -6 to 6
Outputs:
- refreshed: bfloat16 [16, 64, 3584], P('ep', 'dp')
- router_grad: bfloat16 [4096, 384], P(('ep', 'dp'))
The draws below stay inside these ranges and needn't reach their ends.
Inputs may be any that keep to these rules, and one draw needn't show every extreme that they name: `expert_ids`: each row names 2 different experts; among the 128 rows of one device no expert is named more than 24 times, a bound that some block reaches.
All inputs are finite; a program needn't handle non-finite values.
Results may differ from the reference program's by a relative error of at most 0.014.
Values may be sent and summed in bfloat16 or wider, within the bound.
A program may use at most 64 MiB of HBM per device.

```python
import math
import jax
import jax.numpy as jnp
import numpy as np
from jax import lax

D = 3584
FF = 1024
ROUTER = 384
TOPW = 2
TOK_DEV = 128
NEXT = 32
EXPERTS = 16
CAP = 24
TOKENS = 4096
N_EP = 16
N_DP = 2


def draw_router_logits(key, part):
    base_key = jax.random.fold_in(key, 0)
    return (3.0 * jax.random.truncated_normal(base_key, -5.0, 5.0, (TOKENS, ROUTER), jnp.float32)).astype(jnp.bfloat16)


def block_levels(key, dims, pieces, least, largest):
    def one(dim, parts):
        steps = jax.random.uniform(jax.random.fold_in(jax.random.fold_in(key, 6), dim), (parts,), jnp.float32, least / len(pieces), largest / len(pieces))
        return jnp.repeat(jnp.exp(steps), dims[dim] // parts).reshape((-1,) + (1,) * (len(dims) - dim - 1))

    factor_of = one(*pieces[0])
    for cut in pieces[1:]:
        factor_of = factor_of * one(*cut)
    return factor_of


def assign_block(key, own, number, rows, count, top, most, slope):
    sequence = jax.random.permutation(key, count)
    heavy_load, common = portions_of(count, rows * top, most, slope, True), portions_of(count, rows * top, most, slope, False)
    places = jnp.arange(count)

    def named(lengths, offset_by):
        used = int((lengths > 0).sum())
        fixed = max(1, used // 4)
        shifted = fixed + (places - fixed + offset_by * (used - fixed)) % max(1, count - fixed)
        return jnp.zeros((count,), jnp.int32).at[sequence[jnp.where(places < fixed, places, shifted)]].set(jnp.asarray(lengths, jnp.int32))

    lengths = jnp.where(number % 4 == 0, named(heavy_load, number // 4), named(common, number - number // 4 - 1))
    mixed = jax.random.permutation(jax.random.fold_in(own, 3), count)
    source_of, receiver = mixed[0:count // 2 * 2:2], mixed[1:count // 2 * 2:2]
    room = jnp.minimum(lengths[source_of] - 1, most - lengths[receiver]) // 2
    room = jnp.where((source_of == sequence[0]) | (receiver == sequence[0]) | (lengths[receiver] == 0), 0, jnp.maximum(room, 0))
    shifted = jax.random.randint(jax.random.fold_in(own, 4), (count // 2,), 0, 1 << 20) % (room + 1)
    lengths = lengths.at[source_of].add(-shifted).at[receiver].add(shifted)
    members = jnp.searchsorted(jnp.cumsum(lengths), jnp.arange(rows * top), side="right").astype(jnp.int32)
    table = members.reshape(top, rows).T
    table = table[jax.random.permutation(jax.random.fold_in(own, 1), rows)]
    offset_by = jax.random.randint(jax.random.fold_in(own, 2), (rows, 1), 0, top)
    return jnp.take_along_axis(table, (jnp.arange(top)[None, :] + offset_by) % top, axis=1)


def portions_of(amount, total, limit, slope, full):
    portions = [(1 << 20) // math.isqrt(rank ** slope) + 1 for rank in range(1, amount + 1)]
    largest = limit if full else min(limit, max(-(-total // amount), total * portions[0] // sum(portions)))
    least = 1 if total - largest >= amount - 1 else 0
    holding, spare = [largest] + [least] * (amount - 1), total - largest - least * (amount - 1)
    while spare > 0:
        movable = [i for i in range(1, amount) if holding[i] < largest] or [i for i in range(1, amount) if holding[i] < limit]
        pool, left = sum([portions[i] for i in movable]), spare
        for i in movable:
            addition = min(limit - holding[i], max(1, left * portions[i] // pool), spare)
            holding[i] = holding[i] + addition
            spare = spare - addition
    return np.array(holding)


def noise(rng, extent, scale, bound, shards=(), kind=jnp.bfloat16):
    values = scale * jax.random.normal(rng, extent, jnp.float32)
    if shards:
        values = values * block_levels(rng, extent, shards, -0.22, 0.18)
    return jnp.clip(values, -bound, bound).astype(kind)


def setup_inputs(seed: int = 0) -> dict:
    key_list = jax.random.split(jax.random.key(seed), 10)
    out_grad = noise(key_list[0], (TOKENS, D), 1.0, 6.0, ((0, 32),))
    expert_ids_keys = jax.random.split(jax.random.fold_in(key_list[1], 1), TOKENS // TOK_DEV)
    expert_ids_turns = jax.random.permutation(jax.random.fold_in(key_list[1], 3), TOKENS // TOK_DEV)
    expert_ids = jax.vmap(lambda own, number: assign_block(jax.random.fold_in(key_list[1], 2), own, number, TOK_DEV, EXPERTS, TOPW, CAP, 2))(expert_ids_keys, expert_ids_turns).reshape((TOKENS, TOPW))
    combine = jnp.clip(0.1 + 0.9 * jax.random.uniform(key_list[2], (TOKENS, TOPW), jnp.float32) ** block_levels(key_list[2], (TOKENS, TOPW), ((0, 32),), -0.2, 0.2), 0.1, 1.0)
    router_logits = draw_router_logits(jax.random.fold_in(key_list[9], 71), 0)
    saved_hidden = noise(key_list[4], (EXPERTS, N_DP * N_EP * CAP, FF), 1.0, 6.0, ((0, 16), (1, 2)))
    weight = noise(key_list[5], (EXPERTS, FF, D), FF ** -0.5, 0.1875, ((0, 16), (1, 2)))
    moment_one = noise(key_list[6], (EXPERTS, FF, D), 1.0, 6.0, ((0, 16), (1, 2)))
    moment_two = jnp.clip(jnp.exp(math.log(40.0) - 2.9957323 * jax.random.uniform(key_list[7], (EXPERTS, FF, D), jnp.float32) ** block_levels(key_list[7], (EXPERTS, FF, D), ((0, 16), (1, 2)), -0.2, 0.2)), 2.0, 40.0).astype(jnp.bfloat16)
    next_hidden = noise(key_list[8], (EXPERTS, N_DP * NEXT, FF), 1.0, 6.0, ((0, 16), (1, 2)))
    return dict(out_grad=out_grad, expert_ids=expert_ids, combine=combine, router_logits=router_logits, saved_hidden=saved_hidden, weight=weight, moment_one=moment_one, moment_two=moment_two, next_hidden=next_hidden)


beta_one = 0.9
beta_two = 0.95
learn_rate = 0.2
decay_rate = 0.1
step_count = 100.0
adam_eps = 1e-08
zloss_coef = 0.25

def adamw(weight, first, second, gradient):
    first_new = beta_one * first.astype(jnp.float32) + (1.0 - beta_one) * gradient
    second_new = beta_two * second.astype(jnp.float32) + (1.0 - beta_two) * gradient * gradient
    first_hat = first_new / (1.0 - beta_one ** step_count)
    second_hat = second_new / (1.0 - beta_two ** step_count)
    current = weight.astype(jnp.float32)
    change = first_hat / (jnp.sqrt(second_hat) + adam_eps) + decay_rate * current
    return (current - learn_rate * change).astype(jnp.bfloat16)

def zloss_grad(logits):
    values = logits.astype(jnp.float32)
    row_max = lax.optimization_barrier(jnp.max(values, axis=-1, keepdims=True))
    log_total = row_max + jnp.log(lax.optimization_barrier(jnp.sum(jnp.exp(values - row_max), axis=-1, keepdims=True)))
    probs = jnp.exp(values - log_total)
    return (zloss_coef * 2.0 * log_total * probs).astype(jnp.bfloat16)

def reference(out_grad, expert_ids, combine, router_logits, saved_hidden, weight, moment_one, moment_two, next_hidden):
    blocks = TOKENS // TOK_DEV
    per_block = TOK_DEV * TOPW
    ids_block = expert_ids.reshape(blocks, per_block)
    onehot = (ids_block[:, :, None] == jnp.arange(EXPERTS, dtype=jnp.int32)[None, None, :]).astype(jnp.int32)
    before = jnp.cumsum(onehot, axis=1) - onehot
    slot_index = lax.optimization_barrier(jnp.sum(before * onehot, axis=2))
    block_index = jnp.arange(blocks, dtype=jnp.int32)[:, None]
    source = block_index // N_DP
    replica = block_index % N_DP
    row_index = replica * (N_EP * CAP) + source * CAP + slot_index
    total_pos = TOKENS * TOPW
    positions = jnp.arange(total_pos, dtype=jnp.int32)
    table = jnp.full((EXPERTS, N_DP * N_EP * CAP), total_pos, dtype=jnp.int32)
    table = table.at[expert_ids.reshape(-1), row_index.reshape(-1)].set(positions)

    def per_expert(expert):
        position = table[expert]
        valid = position < total_pos
        safe = jnp.minimum(position, total_pos - 1)
        token_index = safe // TOPW
        pick_index = safe % TOPW
        rows = out_grad[token_index].astype(jnp.float32)
        factor = combine[token_index, pick_index]
        sent = jnp.where(valid[:, None], factor[:, None] * rows, 0.0).astype(jnp.bfloat16)
        hidden = saved_hidden[expert].astype(jnp.float32).reshape(N_DP, N_EP * CAP, FF)
        sent_rows = sent.astype(jnp.float32).reshape(N_DP, N_EP * CAP, D)
        partial_value = jnp.einsum('jrf,jrd->jfd', hidden, sent_rows)
        rounded = lax.optimization_barrier(partial_value.astype(jnp.bfloat16))
        gradient = lax.optimization_barrier(jnp.sum(rounded.astype(jnp.float32), axis=0))
        updated = adamw(weight[expert], moment_one[expert], moment_two[expert], gradient)
        return jnp.dot(next_hidden[expert], updated, preferred_element_type=jnp.float32).astype(jnp.bfloat16)
    refreshed = lax.map(per_expert, jnp.arange(EXPERTS, dtype=jnp.int32))
    return (refreshed, zloss_grad(router_logits))
```

```python
import jax
import jax.numpy as jnp
from jax import lax
from jax.sharding import PartitionSpec as P

beta_one = 0.9
beta_two = 0.95
learn_rate = 0.2
decay_rate = 0.1
step_count = 100.0
adam_eps = 1e-08
zloss_coef = 0.25


def adamw(weight, first, second, gradient):
    first_new = beta_one * first.astype(jnp.float32) + (1.0 - beta_one) * gradient
    second_new = beta_two * second.astype(jnp.float32) + (1.0 - beta_two) * gradient * gradient
    first_hat = first_new / (1.0 - beta_one**step_count)
    second_hat = second_new / (1.0 - beta_two**step_count)
    current = weight.astype(jnp.float32)
    change = first_hat / (jnp.sqrt(second_hat) + adam_eps) + decay_rate * current
    return (current - learn_rate * change).astype(jnp.bfloat16)


def zloss_grad(logits):
    values = logits.astype(jnp.float32)
    row_max = jnp.max(values, axis=-1, keepdims=True)
    log_total = row_max + jnp.log(jnp.sum(jnp.exp(values - row_max), axis=-1, keepdims=True))
    probs = jnp.exp(values - log_total)
    return (zloss_coef * 2.0 * log_total * probs).astype(jnp.bfloat16)


def per_device(
    out_grad,
    expert_ids,
    combine,
    router_logits,
    saved_hidden,
    weight,
    moment_one,
    moment_two,
    next_hidden,
):
    experts_count = lax.axis_size("ep")
    replicas = lax.axis_size("dp")
    rows_total = saved_hidden.shape[1]
    capacity = rows_total // experts_count
    model_width = out_grad.shape[1]
    slab_rows = weight.shape[1]
    flat_ids = expert_ids.reshape(-1)
    onehot = (flat_ids[:, None] == jnp.arange(experts_count, dtype=jnp.int32)[None, :]).astype(
        jnp.int32
    )
    before = jnp.cumsum(onehot, axis=0) - onehot
    slot_index = jnp.sum(before * onehot, axis=1)
    target = flat_ids * capacity + slot_index
    scaled = (combine[:, :, None] * out_grad[:, None, :].astype(jnp.float32)).astype(jnp.bfloat16)
    scaled = scaled.reshape(-1, model_width)
    send_rows = jnp.zeros((rows_total, model_width), jnp.bfloat16).at[target].set(scaled)
    received = lax.all_to_all(
        send_rows.reshape(experts_count, capacity, model_width),
        "ep",
        split_axis=0,
        concat_axis=0,
        tiled=True,
    )
    received = received.reshape(rows_total, model_width)
    router_grad = zloss_grad(router_logits)
    if replicas == 2:
        hidden_parts = saved_hidden[0].reshape(rows_total, replicas, slab_rows).swapaxes(0, 1)
        hidden_parts = lax.all_to_all(hidden_parts, "dp", split_axis=0, concat_axis=0, tiled=True)
        me = lax.axis_index("dp")
        other_rows = lax.ppermute(received, "dp", [(0, 1), (1, 0)])
        own_hidden = lax.dynamic_index_in_dim(hidden_parts, me, 0, keepdims=False)
        other_hidden = lax.dynamic_index_in_dim(hidden_parts, 1 - me, 0, keepdims=False)
        gradient = lax.dot_general(
            own_hidden, received, (((0,), (0,)), ((), ())), preferred_element_type=jnp.float32
        ) + lax.dot_general(
            other_hidden, other_rows, (((0,), (0,)), ((), ())), preferred_element_type=jnp.float32
        )
    else:
        partial_value = lax.dot_general(
            saved_hidden[0], received, (((0,), (0,)), ((), ())), preferred_element_type=jnp.float32
        )
        slabs = partial_value.astype(jnp.bfloat16).reshape(replicas, slab_rows, model_width)
        collected = lax.all_to_all(slabs, "dp", split_axis=0, concat_axis=0, tiled=True)
        gradient = jnp.sum(collected.astype(jnp.float32), axis=0)
    updated = adamw(weight[0], moment_one[0], moment_two[0], gradient)
    next_rows = next_hidden.shape[1]
    hidden_slabs = next_hidden[0].reshape(next_rows, replicas, slab_rows).swapaxes(0, 1)
    hidden_slabs = lax.all_to_all(hidden_slabs, "dp", split_axis=0, concat_axis=0, tiled=True)
    product = jnp.dot(
        hidden_slabs.reshape(replicas * next_rows, slab_rows),
        updated,
        preferred_element_type=jnp.float32,
    )
    product = product.astype(jnp.bfloat16).reshape(replicas, next_rows, model_width)
    product = lax.all_to_all(product, "dp", split_axis=0, concat_axis=0, tiled=True)
    refreshed = jnp.sum(product.astype(jnp.float32), axis=0)
    return (refreshed.astype(jnp.bfloat16)[None], router_grad)


def solution(mesh):
    in_specs = (
        P(("ep", "dp"), None),
        P(("ep", "dp"), None),
        P(("ep", "dp"), None),
        P(("ep", "dp"), None),
        P("ep", "dp", None),
        P("ep", "dp", None),
        P("ep", "dp", None),
        P("ep", "dp", None),
        P("ep", "dp", None),
    )
    out_specs = (P("ep", "dp", None), P(("ep", "dp"), None))
    return jax.shard_map(
        per_device, mesh=mesh, in_specs=in_specs, out_specs=out_specs, check_vma=False
    )
```

```python
import functools

import jax
import jax.numpy as jnp
from jax import lax
from jax.experimental import pallas as pl
from jax.experimental.pallas import tpu as pltpu
from jax.sharding import PartitionSpec as P

beta_one = 0.9
beta_two = 0.95
learn_rate = 0.2
decay_rate = 0.1
step_count = 100.0
adam_eps = 1e-08
zloss_coef = 0.25


def adamw(weight, first, second, gradient):
    first_new = beta_one * first.astype(jnp.float32) + (1.0 - beta_one) * gradient
    second_new = beta_two * second.astype(jnp.float32) + (1.0 - beta_two) * gradient * gradient
    first_hat = first_new / (1.0 - beta_one**step_count)
    second_hat = second_new / (1.0 - beta_two**step_count)
    current = weight.astype(jnp.float32)
    change = first_hat / (jnp.sqrt(second_hat) + adam_eps) + decay_rate * current
    return (current - learn_rate * change).astype(jnp.bfloat16)


def zloss_grad(logits):
    values = logits.astype(jnp.float32)
    row_max = jnp.max(values, axis=-1, keepdims=True)
    log_total = row_max + jnp.log(jnp.sum(jnp.exp(values - row_max), axis=-1, keepdims=True))
    probs = jnp.exp(values - log_total)
    return (zloss_coef * 2.0 * log_total * probs).astype(jnp.bfloat16)


def per_device(
    out_grad,
    expert_ids,
    combine,
    router_logits,
    saved_hidden,
    weight,
    moment_one,
    moment_two,
    next_hidden,
):
    experts_count = lax.axis_size("ep")
    replicas = lax.axis_size("dp")
    rows_total = saved_hidden.shape[1]
    capacity = rows_total // experts_count
    model_width = out_grad.shape[1]
    slab_rows = weight.shape[1]
    flat_ids = expert_ids.reshape(-1)
    onehot = (flat_ids[:, None] == jnp.arange(experts_count, dtype=jnp.int32)[None, :]).astype(
        jnp.int32
    )
    before = jnp.cumsum(onehot, axis=0) - onehot
    slot_index = jnp.sum(before * onehot, axis=1)
    target = flat_ids * capacity + slot_index
    scaled = (combine[:, :, None] * out_grad[:, None, :].astype(jnp.float32)).astype(jnp.bfloat16)
    scaled = scaled.reshape(-1, model_width)
    send_rows = jnp.zeros((rows_total, model_width), jnp.bfloat16).at[target].set(scaled)
    received = lax.all_to_all(
        send_rows.reshape(experts_count, capacity, model_width),
        "ep",
        split_axis=0,
        concat_axis=0,
        tiled=True,
    )
    received = received.reshape(rows_total, model_width)
    router_grad = zloss_grad(router_logits)
    if replicas == 2:
        hidden_parts = saved_hidden[0].reshape(rows_total, replicas, slab_rows).swapaxes(0, 1)
        hidden_parts = lax.all_to_all(hidden_parts, "dp", split_axis=0, concat_axis=0, tiled=True)
        me = lax.axis_index("dp")
        other_rows = lax.ppermute(received, "dp", [(0, 1), (1, 0)])
        own_hidden = lax.dynamic_index_in_dim(hidden_parts, me, 0, keepdims=False)
        other_hidden = lax.dynamic_index_in_dim(hidden_parts, 1 - me, 0, keepdims=False)
        gradient = lax.dot_general(
            own_hidden, received, (((0,), (0,)), ((), ())), preferred_element_type=jnp.float32
        ) + lax.dot_general(
            other_hidden, other_rows, (((0,), (0,)), ((), ())), preferred_element_type=jnp.float32
        )
    else:
        partial_value = lax.dot_general(
            saved_hidden[0], received, (((0,), (0,)), ((), ())), preferred_element_type=jnp.float32
        )
        slabs = partial_value.astype(jnp.bfloat16).reshape(replicas, slab_rows, model_width)
        collected = lax.all_to_all(slabs, "dp", split_axis=0, concat_axis=0, tiled=True)
        gradient = jnp.sum(collected.astype(jnp.float32), axis=0)
    updated = adamw(weight[0], moment_one[0], moment_two[0], gradient)
    next_rows = next_hidden.shape[1]
    hidden_slabs = next_hidden[0].reshape(next_rows, replicas, slab_rows).swapaxes(0, 1)
    hidden_slabs = lax.all_to_all(hidden_slabs, "dp", split_axis=0, concat_axis=0, tiled=True)
    product = jnp.dot(
        hidden_slabs.reshape(replicas * next_rows, slab_rows),
        updated,
        preferred_element_type=jnp.float32,
    )
    product = product.astype(jnp.bfloat16).reshape(replicas, next_rows, model_width)
    product = lax.all_to_all(product, "dp", split_axis=0, concat_axis=0, tiled=True)
    refreshed = jnp.sum(product.astype(jnp.float32), axis=0)
    return (refreshed.astype(jnp.bfloat16)[None], router_grad)


MESH = pl.DeviceIdType.MESH


def fused_kernel(
    chunks,
    grad_ref,
    ids_ref,
    combine_ref,
    logits_ref,
    hidden_hbm,
    weight_hbm,
    first_hbm,
    second_hbm,
    next_hbm,
    refreshed_ref,
    router_ref,
    send,
    rows,
    hidden,
    hidden_t,
    weight,
    first,
    second,
    following,
    picks,
    factors,
    gradient,
    updated,
    product_own,
    product_send,
    product_recv,
    send_sem,
    recv_sem,
    pass_send_sem,
    pass_recv_sem,
    local_sem,
    own_sem,
    side_send_sem,
    side_recv_sem,
    product_send_sem,
    product_recv_sem,
):
    experts = send.shape[1]
    capacity = send.shape[2]
    width = send.shape[3]
    slab = weight.shape[0]
    tokens = grad_ref.shape[0]
    count = experts * capacity
    next_rows = following.shape[1]
    groups = experts // 4
    me = lax.axis_index("ep")
    lane = lax.axis_index("dp")
    other = 1 - lane
    group, place = me // 4, me % 4

    barrier = pltpu.get_barrier_semaphore()

    @pl.loop(1, experts)
    def _(step):
        pl.semaphore_signal(
            barrier, inc=1, device_id=((me + step) % experts, lane), device_id_type=MESH
        )

    pl.semaphore_signal(barrier, inc=1, device_id=(me, other), device_id_type=MESH)

    own_columns = pl.ds(pl.multiple_of(lane * slab, slab), slab)
    other_columns = pl.ds(pl.multiple_of(other * slab, slab), slab)
    loads = [
        pltpu.make_async_copy(hidden_hbm.at[:, own_columns], hidden.at[0], local_sem.at[0]),
        pltpu.make_async_copy(next_hbm.at[:, own_columns], following.at[0], local_sem.at[1]),
        pltpu.make_async_copy(weight_hbm, weight, local_sem.at[2]),
        pltpu.make_async_copy(first_hbm, first, local_sem.at[3]),
        pltpu.make_async_copy(second_hbm, second, local_sem.at[4]),
    ]
    for load in loads:
        load.start()

    ids = ids_ref[...]
    weights = combine_ref[...]
    expert_of = lax.broadcasted_iota(jnp.int32, (experts, tokens), 0)
    named = [(ids[k : k + 1, :] == expert_of) for k in range(ids.shape[0])]
    chosen = sum(jnp.where(hit, 1.0, 0.0) for hit in named)
    factor_of = sum(jnp.where(hit, weights[k : k + 1, :], 0.0) for k, hit in enumerate(named))
    earlier = lax.broadcasted_iota(jnp.int32, (tokens, tokens), 0) < lax.broadcasted_iota(
        jnp.int32, (tokens, tokens), 1
    )
    before = jnp.dot(
        chosen.astype(jnp.bfloat16),
        jnp.where(earlier, 1.0, 0.0).astype(jnp.bfloat16),
        preferred_element_type=jnp.float32,
    )
    before = jnp.where(chosen > 0.5, before, -1.0)
    slot = lax.broadcasted_iota(jnp.int32, (capacity, tokens), 0).astype(jnp.float32)
    for e in range(experts):
        pick = jnp.where(before[e : e + 1, :] == slot, 1.0, 0.0)
        picks[e * capacity : (e + 1) * capacity, :] = pick
        factors[e * capacity : (e + 1) * capacity, :] = jnp.broadcast_to(
            jnp.sum(pick * factor_of[e : e + 1, :], axis=1, keepdims=True), (capacity, 128)
        )

    def peer(step):
        return ((group + step // 4) % groups) * 4 + (place + step) % 4

    def source(step):
        return ((group + groups - step // 4) % groups) * 4 + (place + 4 - step % 4) % 4

    def order(step):
        return (step + experts // 2) % experts

    def routed(c, step):
        to = peer(step)
        return pltpu.make_async_remote_copy(
            src_ref=send.at[c, to],
            dst_ref=rows.at[c, me],
            send_sem=send_sem.at[c, step],
            recv_sem=recv_sem.at[c, step],
            device_id=(to, lane),
            device_id_type=MESH,
        )

    def passed(c, step, src):
        return pltpu.make_async_remote_copy(
            src_ref=src,
            dst_ref=rows.at[c, experts + source(step)],
            send_sem=pass_send_sem.at[c, step],
            recv_sem=pass_recv_sem.at[c, step],
            device_id=(me, other),
            device_id_type=MESH,
        )

    sides = [
        pltpu.make_async_remote_copy(
            src_ref=src.at[:, other_columns],
            dst_ref=dst.at[1],
            send_sem=side_send_sem.at[i],
            recv_sem=side_recv_sem.at[i],
            device_id=(me, other),
            device_id_type=MESH,
        )
        for i, (src, dst) in enumerate(((hidden_hbm, hidden), (next_hbm, following)))
    ]

    chosen_rows = picks[...].astype(jnp.bfloat16)
    factor = factors[:, 0:1]

    def own_copy(c):
        return pltpu.make_async_copy(send.at[c, me], rows.at[c, me], own_sem.at[c])

    for c in range(chunks):
        picked = jnp.dot(
            chosen_rows,
            grad_ref[:, c * width : (c + 1) * width],
            preferred_element_type=jnp.float32,
        )
        send[c] = (picked * factor).reshape(experts, capacity, width).astype(jnp.bfloat16)
        if c == 0:
            pl.semaphore_wait(barrier, experts)

        @pl.loop(0, experts)
        def _(index):
            step = order(index)

            @pl.when(step != 0)
            def _():
                routed(c, step).start()

        passed(c, 0, send.at[c, me]).start()
        own_copy(c).start()
        if c == 0:
            for side in sides:
                side.start()

    logits = logits_ref[...].astype(jnp.float32)
    row_max = jnp.max(logits, axis=-1, keepdims=True)
    log_total = row_max + jnp.log(jnp.sum(jnp.exp(logits - row_max), axis=-1, keepdims=True))
    router_ref[...] = (zloss_coef * 2.0 * log_total * jnp.exp(logits - log_total)).astype(
        jnp.bfloat16
    )
    for load in loads:
        load.wait()
    hidden_t[:, 0:count] = hidden[0].astype(jnp.float32).T.astype(jnp.bfloat16)

    def collect(c):
        @pl.loop(0, experts)
        def _(index):
            step = order(index)

            @pl.when(step != 0)
            def _():
                routed(c, step).wait_recv()
                passed(c, step, rows.at[c, source(step)]).start()

        own_copy(c).wait()

    def finish(c):
        @pl.loop(0, experts)
        def _(step):
            passed(c, step, rows.at[c, source(step)]).wait_recv()

        columns = slice(c * width, (c + 1) * width)
        gradient[...] = jnp.dot(
            hidden_t[...],
            rows[c].reshape(2 * count, width),
            preferred_element_type=jnp.float32,
        )

        @pl.loop(0, slab // 16)
        def _(block):
            part = pl.ds(pl.multiple_of(block * 16, 16), 16)
            slope = gradient[part, :]
            first_new = beta_one * first[part, columns].astype(jnp.float32) + (
                1.0 - beta_one
            ) * slope
            second_new = beta_two * second[part, columns].astype(jnp.float32) + (
                1.0 - beta_two
            ) * slope * slope
            first_hat = first_new * (1.0 / (1.0 - beta_one**step_count))
            second_hat = second_new * (1.0 / (1.0 - beta_two**step_count))
            current = weight[part, columns].astype(jnp.float32)
            change = first_hat / (jnp.sqrt(second_hat) + adam_eps) + decay_rate * current
            updated[part, :] = (current - learn_rate * change).astype(jnp.bfloat16)

        product = jnp.dot(
            following[...].reshape(2 * next_rows, slab),
            updated[...],
            preferred_element_type=jnp.float32,
        )
        product_own[c] = product[:next_rows]
        product_send[c] = product[next_rows:].astype(jnp.bfloat16)
        shared(c).start()

    def shared(c):
        return pltpu.make_async_remote_copy(
            src_ref=product_send.at[c],
            dst_ref=product_recv.at[c],
            send_sem=product_send_sem.at[c],
            recv_sem=product_recv_sem.at[c],
            device_id=(me, other),
            device_id_type=MESH,
        )

    collect(0)
    for side in sides:
        side.wait()
    hidden_t[:, count : 2 * count] = hidden[1].astype(jnp.float32).T.astype(jnp.bfloat16)
    for c in range(chunks):
        if c + 1 < chunks:
            collect(c + 1)
        finish(c)

    for c in range(chunks):
        shared(c).wait()
        refreshed_ref[:, c * width : (c + 1) * width] = (
            product_own[c] + product_recv[c].astype(jnp.float32)
        ).astype(jnp.bfloat16)

        @pl.loop(0, experts)
        def _(step):
            @pl.when(step != 0)
            def _():
                routed(c, step).wait_send()

            passed(c, step, rows.at[c, source(step)]).wait_send()


def fused(
    out_grad,
    expert_ids,
    combine,
    router_logits,
    saved_hidden,
    weight,
    moment_one,
    moment_two,
    next_hidden,
):
    experts = lax.axis_size("ep")
    count, _ = saved_hidden.shape[1:]
    capacity = count // experts
    tokens, model_width = out_grad.shape
    slab = weight.shape[1]
    next_rows = next_hidden.shape[1]
    chunks = 4
    width = model_width // chunks
    vmem = pl.BlockSpec(memory_space=pltpu.VMEM)
    hbm = pl.BlockSpec(memory_space=pl.ANY)
    dma = pltpu.SemaphoreType.DMA
    flops = 2 * slab * 2 * count * model_width + 4 * next_rows * slab * model_width
    refreshed, router_grad = pl.pallas_call(
        functools.partial(fused_kernel, chunks),
        out_shape=(
            jax.ShapeDtypeStruct((next_rows, model_width), jnp.bfloat16),
            jax.ShapeDtypeStruct(router_logits.shape, jnp.bfloat16),
        ),
        in_specs=[vmem] * 4 + [hbm] * 5,
        out_specs=(vmem, vmem),
        scratch_shapes=[
            pltpu.VMEM((chunks, experts, capacity, width), jnp.bfloat16),
            pltpu.VMEM((chunks, 2 * experts, capacity, width), jnp.bfloat16),
            pltpu.VMEM((2, count, slab), jnp.bfloat16),
            pltpu.VMEM((slab, 2 * count), jnp.bfloat16),
            pltpu.VMEM((slab, model_width), jnp.bfloat16),
            pltpu.VMEM((slab, model_width), jnp.bfloat16),
            pltpu.VMEM((slab, model_width), jnp.bfloat16),
            pltpu.VMEM((2, next_rows, slab), jnp.bfloat16),
            pltpu.VMEM((count, tokens), jnp.float32),
            pltpu.VMEM((count, 128), jnp.float32),
            pltpu.VMEM((slab, width), jnp.float32),
            pltpu.VMEM((slab, width), jnp.bfloat16),
            pltpu.VMEM((chunks, next_rows, width), jnp.float32),
            pltpu.VMEM((chunks, next_rows, width), jnp.bfloat16),
            pltpu.VMEM((chunks, next_rows, width), jnp.bfloat16),
            dma((chunks, experts)),
            dma((chunks, experts)),
            dma((chunks, experts)),
            dma((chunks, experts)),
            dma((5,)),
            dma((chunks,)),
            dma((2,)),
            dma((2,)),
            dma((chunks,)),
            dma((chunks,)),
        ],
        compiler_params=pltpu.CompilerParams(
            collective_id=0, has_side_effects=True, vmem_limit_bytes=58 * 2**20
        ),
        cost_estimate=pl.CostEstimate(
            flops=flops, bytes_accessed=8 * slab * model_width, transcendentals=0
        ),
        name="fused_expert_step",
    )(
        out_grad,
        expert_ids.T,
        combine.T,
        router_logits,
        saved_hidden[0],
        weight[0],
        moment_one[0],
        moment_two[0],
        next_hidden[0],
    )
    return refreshed[None], router_grad


def fits(mesh, saved_hidden, weight, out_grad):
    experts, replicas = mesh.shape["ep"], mesh.shape["dp"]
    capacity = saved_hidden.shape[1] // (experts * replicas)
    return (
        replicas == 2
        and experts % 4 == 0
        and capacity % 8 == 0
        and (weight.shape[1] // replicas) % 128 == 0
        and out_grad.shape[1] % 512 == 0
    )


def solution(mesh):
    in_specs = (
        P(("ep", "dp"), None),
        P(("ep", "dp"), None),
        P(("ep", "dp"), None),
        P(("ep", "dp"), None),
        P("ep", "dp", None),
        P("ep", "dp", None),
        P("ep", "dp", None),
        P("ep", "dp", None),
        P("ep", "dp", None),
    )
    out_specs = (P("ep", "dp", None), P(("ep", "dp"), None))

    def run(*arrays):
        body = fused if fits(mesh, arrays[4], arrays[5], arrays[0]) else per_device
        return jax.shard_map(
            body, mesh=mesh, in_specs=in_specs, out_specs=out_specs, check_vma=False
        )(*arrays)

    return run
```

```python
import functools

import jax
import jax.numpy as jnp
from jax import lax
from jax.experimental import pallas as pl
from jax.experimental.pallas import tpu as pltpu
from jax.sharding import PartitionSpec as P

beta_one = 0.9
beta_two = 0.95
learn_rate = 0.2
decay_rate = 0.1
step_count = 100.0
adam_eps = 1e-08
zloss_coef = 0.25


def adamw(weight, first, second, gradient):
    first_new = beta_one * first.astype(jnp.float32) + (1.0 - beta_one) * gradient
    second_new = beta_two * second.astype(jnp.float32) + (1.0 - beta_two) * gradient * gradient
    first_hat = first_new / (1.0 - beta_one**step_count)
    second_hat = second_new / (1.0 - beta_two**step_count)
    current = weight.astype(jnp.float32)
    change = first_hat / (jnp.sqrt(second_hat) + adam_eps) + decay_rate * current
    return (current - learn_rate * change).astype(jnp.bfloat16)


def zloss_grad(logits):
    values = logits.astype(jnp.float32)
    row_max = jnp.max(values, axis=-1, keepdims=True)
    log_total = row_max + jnp.log(jnp.sum(jnp.exp(values - row_max), axis=-1, keepdims=True))
    probs = jnp.exp(values - log_total)
    return (zloss_coef * 2.0 * log_total * probs).astype(jnp.bfloat16)


def per_device(
    out_grad,
    expert_ids,
    combine,
    router_logits,
    saved_hidden,
    weight,
    moment_one,
    moment_two,
    next_hidden,
):
    experts_count = lax.axis_size("ep")
    replicas = lax.axis_size("dp")
    rows_total = saved_hidden.shape[1]
    capacity = rows_total // experts_count
    model_width = out_grad.shape[1]
    slab_rows = weight.shape[1]
    flat_ids = expert_ids.reshape(-1)
    onehot = (flat_ids[:, None] == jnp.arange(experts_count, dtype=jnp.int32)[None, :]).astype(
        jnp.int32
    )
    before = jnp.cumsum(onehot, axis=0) - onehot
    slot_index = jnp.sum(before * onehot, axis=1)
    target = flat_ids * capacity + slot_index
    scaled = (combine[:, :, None] * out_grad[:, None, :].astype(jnp.float32)).astype(jnp.bfloat16)
    scaled = scaled.reshape(-1, model_width)
    send_rows = jnp.zeros((rows_total, model_width), jnp.bfloat16).at[target].set(scaled)
    received = lax.all_to_all(
        send_rows.reshape(experts_count, capacity, model_width),
        "ep",
        split_axis=0,
        concat_axis=0,
        tiled=True,
    )
    received = received.reshape(rows_total, model_width)
    router_grad = zloss_grad(router_logits)
    if replicas == 2:
        hidden_parts = saved_hidden[0].reshape(rows_total, replicas, slab_rows).swapaxes(0, 1)
        hidden_parts = lax.all_to_all(hidden_parts, "dp", split_axis=0, concat_axis=0, tiled=True)
        me = lax.axis_index("dp")
        other_rows = lax.ppermute(received, "dp", [(0, 1), (1, 0)])
        own_hidden = lax.dynamic_index_in_dim(hidden_parts, me, 0, keepdims=False)
        other_hidden = lax.dynamic_index_in_dim(hidden_parts, 1 - me, 0, keepdims=False)
        gradient = lax.dot_general(
            own_hidden, received, (((0,), (0,)), ((), ())), preferred_element_type=jnp.float32
        ) + lax.dot_general(
            other_hidden, other_rows, (((0,), (0,)), ((), ())), preferred_element_type=jnp.float32
        )
    else:
        partial_value = lax.dot_general(
            saved_hidden[0], received, (((0,), (0,)), ((), ())), preferred_element_type=jnp.float32
        )
        slabs = partial_value.astype(jnp.bfloat16).reshape(replicas, slab_rows, model_width)
        collected = lax.all_to_all(slabs, "dp", split_axis=0, concat_axis=0, tiled=True)
        gradient = jnp.sum(collected.astype(jnp.float32), axis=0)
    updated = adamw(weight[0], moment_one[0], moment_two[0], gradient)
    next_rows = next_hidden.shape[1]
    hidden_slabs = next_hidden[0].reshape(next_rows, replicas, slab_rows).swapaxes(0, 1)
    hidden_slabs = lax.all_to_all(hidden_slabs, "dp", split_axis=0, concat_axis=0, tiled=True)
    product = jnp.dot(
        hidden_slabs.reshape(replicas * next_rows, slab_rows),
        updated,
        preferred_element_type=jnp.float32,
    )
    product = product.astype(jnp.bfloat16).reshape(replicas, next_rows, model_width)
    product = lax.all_to_all(product, "dp", split_axis=0, concat_axis=0, tiled=True)
    refreshed = jnp.sum(product.astype(jnp.float32), axis=0)
    return (refreshed.astype(jnp.bfloat16)[None], router_grad)


MESH = pl.DeviceIdType.MESH


def fused_kernel(
    chunks,
    grad_ref,
    table_ref,
    logits_ref,
    hidden_hbm,
    weight_hbm,
    first_hbm,
    second_hbm,
    next_hbm,
    refreshed_ref,
    router_ref,
    send,
    rows,
    hidden,
    hidden_t,
    weight,
    first,
    second,
    following,
    picks,
    factors,
    peer_picks,
    peer_factors,
    peer_table,
    peer_grad,
    near_send,
    gradient,
    updated,
    product_own,
    product_send,
    product_recv,
    send_sem,
    recv_sem,
    pass_send_sem,
    pass_recv_sem,
    local_sem,
    own_sem,
    side_send_sem,
    side_recv_sem,
    product_send_sem,
    product_recv_sem,
    near_send_sem,
    near_recv_sem,
    near_own_sem,
    raw_send_sem,
    raw_recv_sem,
    table_sem,
):
    experts = send.shape[1]
    capacity = send.shape[2]
    width = send.shape[3]
    slab = weight.shape[0]
    tokens = grad_ref.shape[0]
    count = experts * capacity
    next_rows = following.shape[1]
    half = experts // 2
    me = lax.axis_index("ep")
    lane = lax.axis_index("dp")
    other = 1 - lane
    side, place = me // half, me % half
    near_base = side * half
    far_base = (1 - side) * half

    barrier = pltpu.get_barrier_semaphore()

    @pl.loop(1, experts)
    def _(step):
        pl.semaphore_signal(
            barrier, inc=1, device_id=((me + step) % experts, lane), device_id_type=MESH
        )

    pl.semaphore_signal(barrier, inc=1, device_id=(me, other), device_id_type=MESH)

    own_columns = pl.ds(pl.multiple_of(lane * slab, slab), slab)
    other_columns = pl.ds(pl.multiple_of(other * slab, slab), slab)
    loads = [
        pltpu.make_async_copy(hidden_hbm.at[:, own_columns], hidden.at[0], local_sem.at[0]),
        pltpu.make_async_copy(next_hbm.at[:, own_columns], following.at[0], local_sem.at[1]),
        pltpu.make_async_copy(weight_hbm, weight, local_sem.at[2]),
        pltpu.make_async_copy(first_hbm, first, local_sem.at[3]),
        pltpu.make_async_copy(second_hbm, second, local_sem.at[4]),
    ]
    for load in loads:
        load.start()

    def shift(step):
        return (place + step) % half

    def shift_back(step):
        return (place + half - step) % half

    def routed(c, step, base):
        to = base + shift(step)
        return pltpu.make_async_remote_copy(
            src_ref=send.at[c, to],
            dst_ref=rows.at[c, me],
            send_sem=send_sem.at[c, step],
            recv_sem=recv_sem.at[c, step],
            device_id=(to, lane),
            device_id_type=MESH,
        )

    def near(c, step):
        return pltpu.make_async_remote_copy(
            src_ref=near_send.at[c, shift(step)],
            dst_ref=rows.at[c, experts + me],
            send_sem=near_send_sem.at[c, step],
            recv_sem=near_recv_sem.at[c, step],
            device_id=(near_base + shift(step), lane),
            device_id_type=MESH,
        )

    def passed(c, step):
        origin = far_base + shift_back(step)
        return pltpu.make_async_remote_copy(
            src_ref=rows.at[c, origin],
            dst_ref=rows.at[c, experts + origin],
            send_sem=pass_send_sem.at[c, step],
            recv_sem=pass_recv_sem.at[c, step],
            device_id=(me, other),
            device_id_type=MESH,
        )

    def to_other(src, dst, send_one, recv_one):
        return pltpu.make_async_remote_copy(
            src_ref=src,
            dst_ref=dst,
            send_sem=send_one,
            recv_sem=recv_one,
            device_id=(me, other),
            device_id_type=MESH,
        )

    def raw(c):
        return to_other(
            grad_ref.at[:, c * width : (c + 1) * width],
            peer_grad.at[c],
            raw_send_sem.at[c],
            raw_recv_sem.at[c],
        )

    table_copy = to_other(table_ref, peer_table, table_sem.at[0], table_sem.at[1])
    sides = [
        to_other(src.at[:, other_columns], dst.at[1], side_send_sem.at[i], side_recv_sem.at[i])
        for i, (src, dst) in enumerate(((hidden_hbm, hidden), (next_hbm, following)))
    ]

    def own_copy(c):
        return pltpu.make_async_copy(send.at[c, me], rows.at[c, me], own_sem.at[c])

    def near_own_copy(c):
        return pltpu.make_async_copy(
            near_send.at[c, place], rows.at[c, experts + me], near_own_sem.at[c]
        )

    def make_picks(table, base, wanted, picks_out, factors_out):
        top = table.shape[0] // 2
        expert_of = lax.broadcasted_iota(jnp.int32, (wanted, tokens), 0) + base
        expert_of = expert_of.astype(jnp.float32)
        named = [(table[k : k + 1, :] == expert_of) for k in range(top)]
        chosen = sum(jnp.where(hit, 1.0, 0.0) for hit in named)
        factor_of = sum(
            jnp.where(hit, table[top + k : top + k + 1, :], 0.0) for k, hit in enumerate(named)
        )
        earlier = lax.broadcasted_iota(jnp.int32, (tokens, tokens), 0) < lax.broadcasted_iota(
            jnp.int32, (tokens, tokens), 1
        )
        before = jnp.dot(
            chosen.astype(jnp.bfloat16),
            jnp.where(earlier, 1.0, 0.0).astype(jnp.bfloat16),
            preferred_element_type=jnp.float32,
        )
        before = jnp.where(chosen > 0.5, before, -1.0)
        slot = lax.broadcasted_iota(jnp.int32, (capacity, tokens), 0).astype(jnp.float32)
        for e in range(wanted):
            pick = jnp.where(before[e : e + 1, :] == slot, 1.0, 0.0)
            picks_out[e * capacity : (e + 1) * capacity, :] = pick
            factors_out[e * capacity : (e + 1) * capacity, :] = jnp.broadcast_to(
                jnp.sum(pick * factor_of[e : e + 1, :], axis=1, keepdims=True), (capacity, 128)
            )

    def send_own(c):
        picked = jnp.dot(
            picks[...].astype(jnp.bfloat16),
            grad_ref[:, c * width : (c + 1) * width],
            preferred_element_type=jnp.float32,
        )
        scaled = picked * factors[:, 0:1]
        send[c] = scaled.reshape(experts, capacity, width).astype(jnp.bfloat16)

        @pl.loop(0, half)
        def _(step):
            routed(c, half + step, far_base).start()

        @pl.loop(1, half)
        def _(step):
            routed(c, step, near_base).start()

        own_copy(c).start()

    def send_near(c):
        raw(c).wait_recv()
        picked = jnp.dot(
            peer_picks[...].astype(jnp.bfloat16),
            peer_grad[c],
            preferred_element_type=jnp.float32,
        )
        scaled = picked * peer_factors[:, 0:1]
        near_send[c] = scaled.reshape(half, capacity, width).astype(jnp.bfloat16)

        @pl.loop(1, half)
        def _(step):
            near(c, step).start()

        near_own_copy(c).start()

    def router_part():
        logits = logits_ref[...].astype(jnp.float32)
        row_max = jnp.max(logits, axis=-1, keepdims=True)
        log_total = row_max + jnp.log(jnp.sum(jnp.exp(logits - row_max), axis=-1, keepdims=True))
        router_ref[...] = (zloss_coef * 2.0 * log_total * jnp.exp(logits - log_total)).astype(
            jnp.bfloat16
        )

    def collect(c):
        @pl.loop(0, half)
        def _(step):
            routed(c, half + step, far_base).wait_recv()
            passed(c, step).start()

    def finish(c):
        @pl.loop(1, half)
        def _(step):
            routed(c, step, near_base).wait_recv()
            near(c, step).wait_recv()

        own_copy(c).wait()
        near_own_copy(c).wait()

        @pl.loop(0, half)
        def _(step):
            passed(c, step).wait_recv()

        columns = slice(c * width, (c + 1) * width)
        gradient[...] = jnp.dot(
            hidden_t[...],
            rows[c].reshape(2 * count, width),
            preferred_element_type=jnp.float32,
        )

        @pl.loop(0, slab // 16)
        def _(block):
            part = pl.ds(pl.multiple_of(block * 16, 16), 16)
            slope = gradient[part, :]
            first_new = beta_one * first[part, columns].astype(jnp.float32) + (
                1.0 - beta_one
            ) * slope
            second_new = beta_two * second[part, columns].astype(jnp.float32) + (
                1.0 - beta_two
            ) * slope * slope
            first_hat = first_new * (1.0 / (1.0 - beta_one**step_count))
            second_hat = second_new * (1.0 / (1.0 - beta_two**step_count))
            current = weight[part, columns].astype(jnp.float32)
            change = first_hat / (jnp.sqrt(second_hat) + adam_eps) + decay_rate * current
            updated[part, :] = (current - learn_rate * change).astype(jnp.bfloat16)

        product = jnp.dot(
            following[...].reshape(2 * next_rows, slab),
            updated[...],
            preferred_element_type=jnp.float32,
        )
        product_own[c] = product[:next_rows]
        product_send[c] = product[next_rows:].astype(jnp.bfloat16)
        shared(c).start()

    def shared(c):
        return to_other(
            product_send.at[c], product_recv.at[c], product_send_sem.at[c], product_recv_sem.at[c]
        )

    pl.semaphore_wait(barrier, experts)
    table_copy.start()
    raw(0).start()
    raw(1).start()
    make_picks(table_ref[...], 0, experts, picks, factors)
    send_own(0)
    table_copy.wait_recv()
    make_picks(peer_table[...], near_base, half, peer_picks, peer_factors)
    send_near(0)
    raw(2).start()
    send_own(1)
    router_part()
    send_near(1)
    for c in range(3, chunks):
        raw(c).start()
    for one in sides:
        one.start()
    send_own(2)
    for load in loads:
        load.wait()
    hidden_t[:, 0:count] = hidden[0].astype(jnp.float32).T.astype(jnp.bfloat16)
    collect(0)
    send_near(2)
    for c in range(3, chunks):
        send_own(c)
        send_near(c)
    for one in sides:
        one.wait()
    hidden_t[:, count : 2 * count] = hidden[1].astype(jnp.float32).T.astype(jnp.bfloat16)
    for c in range(chunks):
        if c + 1 < chunks:
            collect(c + 1)
        finish(c)

    table_copy.wait_send()
    for c in range(chunks):
        shared(c).wait()
        refreshed_ref[:, c * width : (c + 1) * width] = (
            product_own[c] + product_recv[c].astype(jnp.float32)
        ).astype(jnp.bfloat16)
        raw(c).wait_send()

        @pl.loop(0, half)
        def _(step):
            routed(c, half + step, far_base).wait_send()
            passed(c, step).wait_send()

        @pl.loop(1, half)
        def _(step):
            routed(c, step, near_base).wait_send()
            near(c, step).wait_send()


def fused(
    out_grad,
    expert_ids,
    combine,
    router_logits,
    saved_hidden,
    weight,
    moment_one,
    moment_two,
    next_hidden,
):
    experts = lax.axis_size("ep")
    count, _ = saved_hidden.shape[1:]
    capacity = count // experts
    tokens, model_width = out_grad.shape
    slab = weight.shape[1]
    next_rows = next_hidden.shape[1]
    chunks = 4
    width = model_width // chunks
    table = jnp.concatenate([expert_ids.T.astype(jnp.float32), combine.T])
    vmem = pl.BlockSpec(memory_space=pltpu.VMEM)
    hbm = pl.BlockSpec(memory_space=pl.ANY)
    dma = pltpu.SemaphoreType.DMA
    flops = 2 * slab * 2 * count * model_width + 4 * next_rows * slab * model_width
    refreshed, router_grad = pl.pallas_call(
        functools.partial(fused_kernel, chunks),
        out_shape=(
            jax.ShapeDtypeStruct((next_rows, model_width), jnp.bfloat16),
            jax.ShapeDtypeStruct(router_logits.shape, jnp.bfloat16),
        ),
        in_specs=[vmem] * 3 + [hbm] * 5,
        out_specs=(vmem, vmem),
        scratch_shapes=[
            pltpu.VMEM((chunks, experts, capacity, width), jnp.bfloat16),
            pltpu.VMEM((chunks, 2 * experts, capacity, width), jnp.bfloat16),
            pltpu.VMEM((2, count, slab), jnp.bfloat16),
            pltpu.VMEM((slab, 2 * count), jnp.bfloat16),
            pltpu.VMEM((slab, model_width), jnp.bfloat16),
            pltpu.VMEM((slab, model_width), jnp.bfloat16),
            pltpu.VMEM((slab, model_width), jnp.bfloat16),
            pltpu.VMEM((2, next_rows, slab), jnp.bfloat16),
            pltpu.VMEM((count, tokens), jnp.float32),
            pltpu.VMEM((count, 128), jnp.float32),
            pltpu.VMEM((count // 2, tokens), jnp.float32),
            pltpu.VMEM((count // 2, 128), jnp.float32),
            pltpu.VMEM(table.shape, jnp.float32),
            pltpu.VMEM((chunks, tokens, width), jnp.bfloat16),
            pltpu.VMEM((chunks, experts // 2, capacity, width), jnp.bfloat16),
            pltpu.VMEM((slab, width), jnp.float32),
            pltpu.VMEM((slab, width), jnp.bfloat16),
            pltpu.VMEM((chunks, next_rows, width), jnp.float32),
            pltpu.VMEM((chunks, next_rows, width), jnp.bfloat16),
            pltpu.VMEM((chunks, next_rows, width), jnp.bfloat16),
            dma((chunks, experts)),
            dma((chunks, experts)),
            dma((chunks, experts // 2)),
            dma((chunks, experts // 2)),
            dma((5,)),
            dma((chunks,)),
            dma((2,)),
            dma((2,)),
            dma((chunks,)),
            dma((chunks,)),
            dma((chunks, experts // 2)),
            dma((chunks, experts // 2)),
            dma((chunks,)),
            dma((chunks,)),
            dma((chunks,)),
            dma((2,)),
        ],
        compiler_params=pltpu.CompilerParams(
            collective_id=0, has_side_effects=True, vmem_limit_bytes=58 * 2**20
        ),
        cost_estimate=pl.CostEstimate(
            flops=flops, bytes_accessed=8 * slab * model_width, transcendentals=0
        ),
        name="fused_expert_step",
    )(
        out_grad,
        table,
        router_logits,
        saved_hidden[0],
        weight[0],
        moment_one[0],
        moment_two[0],
        next_hidden[0],
    )
    return refreshed[None], router_grad


def fits(mesh, saved_hidden, weight, out_grad):
    experts, replicas = mesh.shape["ep"], mesh.shape["dp"]
    capacity = saved_hidden.shape[1] // (experts * replicas)
    return (
        replicas == 2
        and experts % 4 == 0
        and capacity % 8 == 0
        and (weight.shape[1] // replicas) % 128 == 0
        and out_grad.shape[1] % 512 == 0
    )


def solution(mesh):
    in_specs = (
        P(("ep", "dp"), None),
        P(("ep", "dp"), None),
        P(("ep", "dp"), None),
        P(("ep", "dp"), None),
        P("ep", "dp", None),
        P("ep", "dp", None),
        P("ep", "dp", None),
        P("ep", "dp", None),
        P("ep", "dp", None),
    )
    out_specs = (P("ep", "dp", None), P(("ep", "dp"), None))

    def run(*arrays):
        body = fused if fits(mesh, arrays[4], arrays[5], arrays[0]) else per_device
        return jax.shard_map(
            body, mesh=mesh, in_specs=in_specs, out_specs=out_specs, check_vma=False
        )(*arrays)

    return run
```
